32 devices in a mesh: blk: 16 (over z, y, x), grp: 2 (over core).
Axes of the slice: x: 2, y: 2, z: 4, core: 2. Of those that a mesh axis runs over, the one named last changes fastest.
Arguments:
- image_emb: bfloat16 [8192, 1152], P(('blk', 'grp')), may hold values from -8 to 8
- text_emb: bfloat16 [8192, 1152], P(('blk', 'grp')), may hold values from -8 to 8
- log_temp: float32 [1], replicated, may hold values from 1.6 to 2.8
- bias: float32 [1], replicated, may hold values from -3 to -1
Outputs:
- grad_image: float32 [8192, 1152], P(('blk', 'grp'))
- grad_text: float32 [8192, 1152], P(('blk', 'grp'))
- statistics: float32 [3], replicated
The draws below stay inside these ranges and needn't reach their ends.
All inputs are finite; a program needn't handle non-finite values.
Results may differ from the reference program's by a relative error of at most 0.00032.
Values may be sent and summed in bfloat16 or wider, within the bound.
No kernel may reach another device: no remote copies, remote signals or barrier semaphores. Data moves between devices by JAX's collectives and lax.ppermute only.
A program may use at most 64 MiB of HBM per device.

```python
import jax
import jax.numpy as jnp
from jax import lax

D = 1152
ROWS = 256
REACH = 2
TOKENS = 8192
PAIRS = 10485760
N_BLK = 16
N_GRP = 2


def shared_direction(key):
    return jax.random.normal(jax.random.fold_in(key, 101), (D,), jnp.float32)


def embed_rows(noise, direction, amplitude):
    position = (jnp.arange(TOKENS, dtype=jnp.float32) + 0.5) / TOKENS
    rows = noise + amplitude * position[:, None] * direction[None, :]
    return jnp.clip(rows, -8.0, 8.0)


def draw_image_emb(key, part):
    direction = shared_direction(key)
    key = jax.random.fold_in(key, 1)
    noise = jax.random.normal(key, (TOKENS, D), jnp.float32)
    rows = embed_rows(noise, direction, 1.2)
    return rows.astype(jnp.bfloat16)


def draw_text_emb(key, part):
    direction = shared_direction(key)
    key = jax.random.fold_in(key, 2)
    noise = jax.random.normal(key, (TOKENS, D), jnp.float32)
    rows = embed_rows(noise, direction, 1.2)
    return rows.astype(jnp.bfloat16)


def setup_inputs(seed: int = 0) -> dict:
    key_of = jax.random.split(jax.random.key(seed), 5)
    image_emb = draw_image_emb(jax.random.fold_in(key_of[4], 71), 0)
    text_emb = draw_text_emb(jax.random.fold_in(key_of[4], 71), 0)
    log_temp = jnp.clip(jax.random.uniform(key_of[2], (1,), jnp.float32, 1.6, 2.8), 1.6, 2.8)
    bias = jnp.clip(jax.random.uniform(key_of[3], (1,), jnp.float32, -3.0, -1.0), -3.0, -1.0)
    return dict(image_emb=image_emb, text_emb=text_emb, log_temp=log_temp, bias=bias)


def normalize(raw_rows):
    widened = raw_rows.astype(jnp.float32)
    inverse = 1.0 / jnp.sqrt(lax.optimization_barrier(jnp.sum(widened * widened, axis=1, keepdims=True)) + 1e-06)
    return (widened * inverse, inverse)

def reference(image_emb, text_emb, log_temp, bias):
    img_wide, img_inv = normalize(image_emb)
    txt_wide, txt_inv = normalize(text_emb)
    shape4 = (N_BLK, N_GRP, ROWS, D)
    img_unit = img_wide.astype(jnp.bfloat16).astype(jnp.float32).reshape(shape4)
    txt_unit = txt_wide.astype(jnp.bfloat16).astype(jnp.float32).reshape(shape4)
    temper = jnp.exp(log_temp[0])
    offset_bias = bias[0]
    ident = jnp.arange(ROWS)[:, None] == jnp.arange(ROWS)[None, :]
    grad_img = jnp.zeros(shape4, jnp.float32)
    grad_txt = jnp.zeros(shape4, jnp.float32)
    loss_sum = jnp.float32(0.0)
    temp_sum = jnp.float32(0.0)
    bias_sum = jnp.float32(0.0)
    for offset in range(-REACH, REACH + 1):
        visitor = jnp.roll(txt_unit, offset, axis=0)
        similar = jnp.einsum('bgrd,bgqd->bgrq', img_unit, visitor)
        logits = temper * similar + offset_bias
        if offset == 0:
            labels = jnp.where(ident, 1.0, -1.0).astype(jnp.float32)
        else:
            labels = -jnp.ones((ROWS, ROWS), jnp.float32)
        margin = -labels * logits
        loss_sum = loss_sum + jnp.sum(jax.nn.softplus(margin))
        slope = -labels * jax.nn.sigmoid(margin)
        temp_sum = temp_sum + jnp.sum(slope * temper * similar)
        bias_sum = bias_sum + jnp.sum(slope)
        scaled = (temper * slope).astype(jnp.bfloat16).astype(jnp.float32)
        grad_img = grad_img + jnp.einsum('bgrq,bgqd->bgrd', scaled, visitor)
        back = jnp.einsum('bgrq,bgrd->bgqd', scaled, img_unit)
        grad_txt = grad_txt + jnp.roll(back, -offset, axis=0)
    grad_img = grad_img.reshape(TOKENS, D)
    grad_txt = grad_txt.reshape(TOKENS, D)
    grad_image = img_inv * (grad_img - img_wide * lax.optimization_barrier(jnp.sum(img_wide * grad_img, axis=1, keepdims=True)))
    grad_text = txt_inv * (grad_txt - txt_wide * lax.optimization_barrier(jnp.sum(txt_wide * grad_txt, axis=1, keepdims=True)))
    pair_count = jnp.float32(PAIRS)
    statistics = jnp.stack([loss_sum, temp_sum, bias_sum]) / pair_count
    return (grad_image, grad_text, statistics)
```

```python
import functools

import jax
import jax.numpy as jnp
from jax import lax
from jax.experimental import pallas as pl
from jax.experimental.pallas import tpu as pltpu
from jax.sharding import PartitionSpec as P

REACH = 2
QUAD = 4
VMEM_LIMIT = 48 * 1024 * 1024
IN_VMEM = pl.BlockSpec(memory_space=pltpu.VMEM)
IN_SMEM = pl.BlockSpec(memory_space=pltpu.SMEM)


def unit_rows(raw):
    wide = raw.astype(jnp.float32)
    inverse = 1.0 / jnp.sqrt(jnp.sum(wide * wide, axis=1, keepdims=True) + 1e-06)
    return wide * inverse, inverse


def slopes(similar, temper, offset_bias, diagonal):
    logits = temper * similar + offset_bias
    tail = jnp.exp(-jnp.abs(logits))
    upper = jnp.where(logits >= 0, 1.0, tail) / (1.0 + tail)
    if not diagonal:
        return logits, tail, upper, logits
    lower = jnp.where(logits >= 0, tail, 1.0) / (1.0 + tail)
    same = lax.broadcasted_iota(jnp.int32, similar.shape, 0) == lax.broadcasted_iota(
        jnp.int32, similar.shape, 1
    )
    return logits, tail, jnp.where(same, -lower, upper), jnp.where(same, -logits, logits)


def fold(tile):
    rows, columns = tile.shape
    part = jnp.sum(tile.reshape(rows // 8, 8, columns), axis=0)
    return sum(part[:, c : c + 128] for c in range(0, columns, 128))


def tallies(margin, tail, slope, logits_part):
    pair_loss = jnp.maximum(margin, 0.0) + jnp.log1p(tail)
    return jnp.concatenate([fold(pair_loss), fold(slope * logits_part), fold(slope)], axis=0)


def across(left, right):
    return lax.dot_general(
        left, right, (((1,), (1,)), ((), ())), preferred_element_type=jnp.float32
    )


def own_kernel(scalars, image, text, img_unit, txt_unit, img_inv, txt_inv, gx, gy, stats):
    temper, offset_bias = scalars[0], scalars[1]
    x_wide, x_inv = unit_rows(image[...])
    y_wide, y_inv = unit_rows(text[...])
    x, y = x_wide.astype(jnp.bfloat16), y_wide.astype(jnp.bfloat16)
    img_unit[...] = x
    txt_unit[...] = y
    img_inv[...] = jnp.broadcast_to(x_inv, img_inv.shape)
    txt_inv[...] = jnp.broadcast_to(y_inv, txt_inv.shape)
    similar = across(x, y)
    _, tail, slope, margin = slopes(similar, temper, offset_bias, True)
    stats[...] = tallies(margin, tail, slope, temper * similar)
    scaled = (temper * slope).astype(jnp.bfloat16)
    gx[...] = jnp.dot(scaled, y, preferred_element_type=jnp.float32)
    _, _, slope, _ = slopes(across(y, x), temper, offset_bias, True)
    scaled = (temper * slope).astype(jnp.bfloat16)
    gy[...] = jnp.dot(scaled, x, preferred_element_type=jnp.float32)


def visit_kernel(counted, last, *refs):
    refs = list(refs)
    scalars, own, visitor = refs.pop(0), refs.pop(0), refs.pop(0)
    other = refs.pop(0) if last else None
    acc = refs.pop(0)
    stats = refs.pop(0) if counted else None
    raw, inverse = (refs.pop(0), refs.pop(0)) if last else (None, None)
    out = refs.pop(0)
    temper, offset_bias = scalars[0], scalars[1]
    block = visitor[...].astype(jnp.float32)
    if last:
        block = jnp.where(scalars[2] > 0.5, block, other[...].astype(jnp.float32))
    unit = unit_rows(block)[0].astype(jnp.bfloat16)
    similar = across(own[...], unit)
    logits, tail, slope, _ = slopes(similar, temper, offset_bias, False)
    scaled = (temper * slope).astype(jnp.bfloat16)
    grad = acc[...] + jnp.dot(scaled, unit, preferred_element_type=jnp.float32)
    if last:
        inv = inverse[:, :1]
        wide = raw[...].astype(jnp.float32) * inv
        grad = inv * (grad - wide * jnp.sum(wide * grad, axis=1, keepdims=True))
    out[...] = grad
    if counted:
        tally = stats[...] + tallies(logits, tail, slope, temper * similar)
        if last:
            lane = lax.broadcasted_iota(jnp.int32, (8, 128), 1)
            sums = [jnp.sum(tally[8 * i : 8 * i + 8]) for i in range(3)]
            row = jnp.where(lane == 0, sums[0], jnp.where(lane == 1, sums[1], sums[2]))
            refs[0][...] = jnp.broadcast_to(row[None], refs[0].shape)
        else:
            refs[0][...] = tally


def cost(rows, width, tiles):
    return pl.CostEstimate(
        flops=4 * tiles * rows * rows * width,
        bytes_accessed=12 * rows * width,
        transcendentals=tiles * rows * rows,
    )


def call(kernel, operands, shapes, rows, width, tiles):
    return pl.pallas_call(
        kernel,
        out_shape=shapes,
        in_specs=[IN_SMEM] + [IN_VMEM] * (len(operands) - 1),
        out_specs=tuple(IN_VMEM for _ in shapes),
        compiler_params=pltpu.CompilerParams(vmem_limit_bytes=VMEM_LIMIT),
        cost_estimate=cost(rows, width, tiles),
    )(*operands)


def visit(scalars, own, visitor, acc, stats=None, other=None, finish=None, devices=0):
    rows, width = own.shape
    last = finish is not None
    counted = stats is not None
    operands = [scalars, own, visitor]
    if last:
        operands.append(other)
    operands.append(acc)
    if counted:
        operands.append(stats)
    if last:
        operands += list(finish)
    shapes = [jax.ShapeDtypeStruct((rows, width), jnp.float32)]
    if counted:
        shape = (devices, 8, 128) if last else (24, 128)
        shapes.append(jax.ShapeDtypeStruct(shape, jnp.float32))
    return call(functools.partial(visit_kernel, counted, last), operands, tuple(shapes), rows, width, 1)


def on_device(image, text, log_temp, bias):
    rows, width = image.shape
    blocks = lax.axis_size("blk")
    devices = blocks * lax.axis_size("grp")
    place = lax.axis_index("blk") % QUAD
    everyone = range(blocks)
    f32 = jnp.float32
    scalars = jnp.stack(
        [jnp.exp(log_temp[0]), bias[0], jnp.where((place == 0) | (place == 3), 1.0, 0.0).astype(f32)]
    )

    def send(block, route):
        return lax.ppermute(block, "blk", route)

    beside = [(b, b ^ 1) for b in everyone]
    above = [(b, b ^ 2) for b in everyone]
    beyond = [(b, (b + QUAD if b % QUAD < 2 else b - QUAD) % blocks) for b in everyone]
    corner = [(b, b ^ 1) for b in everyone if b % QUAD in (1, 2)]
    middle_x = [(b, b ^ 1) for b in everyone if b % QUAD in (0, 3)]
    middle_y = [(b, b ^ 2) for b in everyone if b % QUAD in (0, 3)]

    txt_y = send(text, above)
    txt_x = send(text, beside)
    img_y = send(image, above)
    img_x = send(image, beside)

    tile = jax.ShapeDtypeStruct((rows, width), f32)
    unit = jax.ShapeDtypeStruct((rows, width), jnp.bfloat16)
    column = jax.ShapeDtypeStruct((rows, 128), f32)
    img_unit, txt_unit, img_inv, txt_inv, gx, gy, stats = call(
        own_kernel,
        [scalars, image, text],
        (unit, unit, column, column, tile, tile, jax.ShapeDtypeStruct((24, 128), f32)),
        rows,
        width,
        2,
    )

    txt_z = send(txt_y, beyond)
    img_z = send(img_y, beyond)
    txt_z, img_x = lax.optimization_barrier((txt_z, img_x))
    txt_c = send(txt_z, corner)
    txt_m = send(txt_y, middle_x)
    img_m = send(img_x, middle_y)
    img_c = send(img_z, corner)

    gx, stats = visit(scalars, img_unit, txt_y, gx, stats)
    gx, stats = visit(scalars, img_unit, txt_x, gx, stats)
    (gy,) = visit(scalars, txt_unit, img_y, gy)
    (gy,) = visit(scalars, txt_unit, img_x, gy)
    gx, stats = visit(scalars, img_unit, txt_z, gx, stats)
    (gy,) = visit(scalars, txt_unit, img_z, gy)
    grad_image, sums = visit(
        scalars, img_unit, txt_c, gx, stats, txt_m, (image, img_inv), devices
    )
    (grad_text,) = visit(scalars, txt_unit, img_c, gy, None, img_m, (text, txt_inv))
    seen = lax.all_to_all(sums, ("blk", "grp"), 0, 0)
    pairs = jnp.float32(rows * rows * (2 * REACH + 1) * devices)
    statistics = jnp.sum(seen[:, 0, :3], axis=0) / pairs
    return grad_image, grad_text, statistics


def solution(mesh):
    placed = P(("blk", "grp"), None)
    return jax.shard_map(
        on_device,
        mesh=mesh,
        in_specs=(placed, placed, P(), P()),
        out_specs=(placed, placed, P()),
        check_vma=False,
    )
```

```python
import functools

import jax
import jax.numpy as jnp
from jax import lax
from jax.experimental import pallas as pl
from jax.experimental.pallas import tpu as pltpu
from jax.sharding import PartitionSpec as P

REACH = 2
QUAD = 4
VMEM_LIMIT = 48 * 1024 * 1024
IN_VMEM = pl.BlockSpec(memory_space=pltpu.VMEM)
IN_SMEM = pl.BlockSpec(memory_space=pltpu.SMEM)


def unit_rows(raw):
    wide = raw.astype(jnp.float32)
    inverse = 1.0 / jnp.sqrt(jnp.sum(wide * wide, axis=1, keepdims=True) + 1e-06)
    return wide * inverse, inverse


def slopes(similar, temper, offset_bias, diagonal):
    logits = temper * similar + offset_bias
    tail = jnp.exp(-jnp.abs(logits))
    upper = jnp.where(logits >= 0, 1.0, tail) / (1.0 + tail)
    if not diagonal:
        return logits, tail, upper, logits
    lower = jnp.where(logits >= 0, tail, 1.0) / (1.0 + tail)
    same = lax.broadcasted_iota(jnp.int32, similar.shape, 0) == lax.broadcasted_iota(
        jnp.int32, similar.shape, 1
    )
    return logits, tail, jnp.where(same, -lower, upper), jnp.where(same, -logits, logits)


def fold(tile):
    rows, columns = tile.shape
    part = jnp.sum(tile.reshape(rows // 8, 8, columns), axis=0)
    return sum(part[:, c : c + 128] for c in range(0, columns, 128))


def tallies(margin, tail, slope, logits_part):
    pair_loss = jnp.maximum(margin, 0.0) + jnp.log1p(tail)
    return jnp.concatenate([fold(pair_loss), fold(slope * logits_part), fold(slope)], axis=0)


def across(left, right):
    return lax.dot_general(
        left, right, (((1,), (1,)), ((), ())), preferred_element_type=jnp.float32
    )


def own_kernel(scalars, image, text, img_unit, txt_unit, img_inv, txt_inv, gx, gy, stats):
    temper, offset_bias = scalars[0], scalars[1]
    x_wide, x_inv = unit_rows(image[...])
    y_wide, y_inv = unit_rows(text[...])
    x, y = x_wide.astype(jnp.bfloat16), y_wide.astype(jnp.bfloat16)
    img_unit[...] = x
    txt_unit[...] = y
    img_inv[...] = jnp.broadcast_to(x_inv, img_inv.shape)
    txt_inv[...] = jnp.broadcast_to(y_inv, txt_inv.shape)
    similar = across(x, y)
    _, tail, slope, margin = slopes(similar, temper, offset_bias, True)
    stats[...] = tallies(margin, tail, slope, temper * similar)
    scaled = (temper * slope).astype(jnp.bfloat16)
    gx[...] = jnp.dot(scaled, y, preferred_element_type=jnp.float32)
    _, _, slope, _ = slopes(across(y, x), temper, offset_bias, True)
    scaled = (temper * slope).astype(jnp.bfloat16)
    gy[...] = jnp.dot(scaled, x, preferred_element_type=jnp.float32)


def visit_kernel(counted, last, *refs):
    refs = list(refs)
    scalars, own, visitor = refs.pop(0), refs.pop(0), refs.pop(0)
    other = refs.pop(0) if last else None
    acc = refs.pop(0)
    stats = refs.pop(0) if counted else None
    raw, inverse = (refs.pop(0), refs.pop(0)) if last else (None, None)
    out = refs.pop(0)
    temper, offset_bias = scalars[0], scalars[1]
    block = visitor[...].astype(jnp.float32)
    if last:
        block = jnp.where(scalars[2] > 0.5, block, other[...].astype(jnp.float32))
    unit = unit_rows(block)[0].astype(jnp.bfloat16)
    similar = across(own[...], unit)
    logits, tail, slope, _ = slopes(similar, temper, offset_bias, False)
    scaled = (temper * slope).astype(jnp.bfloat16)
    grad = acc[...] + jnp.dot(scaled, unit, preferred_element_type=jnp.float32)
    if last:
        inv = inverse[:, :1]
        wide = raw[...].astype(jnp.float32) * inv
        grad = inv * (grad - wide * jnp.sum(wide * grad, axis=1, keepdims=True))
    out[...] = grad
    if counted:
        tally = stats[...] + tallies(logits, tail, slope, temper * similar)
        if last:
            lane = lax.broadcasted_iota(jnp.int32, (8, 128), 1)
            sums = [jnp.sum(tally[8 * i : 8 * i + 8]) for i in range(3)]
            row = jnp.where(lane == 0, sums[0], jnp.where(lane == 1, sums[1], sums[2]))
            refs[0][...] = jnp.broadcast_to(row[None], refs[0].shape)
        else:
            refs[0][...] = tally


def cost(rows, width, tiles):
    return pl.CostEstimate(
        flops=4 * tiles * rows * rows * width,
        bytes_accessed=12 * rows * width,
        transcendentals=tiles * rows * rows,
    )


def call(kernel, operands, shapes, rows, width, tiles):
    return pl.pallas_call(
        kernel,
        out_shape=shapes,
        in_specs=[IN_SMEM] + [IN_VMEM] * (len(operands) - 1),
        out_specs=tuple(IN_VMEM for _ in shapes),
        compiler_params=pltpu.CompilerParams(vmem_limit_bytes=VMEM_LIMIT),
        cost_estimate=cost(rows, width, tiles),
    )(*operands)


def visit(scalars, own, visitor, acc, stats=None, other=None, finish=None, devices=0):
    rows, width = own.shape
    last = finish is not None
    counted = stats is not None
    operands = [scalars, own, visitor]
    if last:
        operands.append(other)
    operands.append(acc)
    if counted:
        operands.append(stats)
    if last:
        operands += list(finish)
    shapes = [jax.ShapeDtypeStruct((rows, width), jnp.float32)]
    if counted:
        shape = (devices, 8, 128) if last else (24, 128)
        shapes.append(jax.ShapeDtypeStruct(shape, jnp.float32))
    return call(functools.partial(visit_kernel, counted, last), operands, tuple(shapes), rows, width, 1)


def tied(*values):
    return lax.optimization_barrier(values)


def on_device(image, text, log_temp, bias):
    rows, width = image.shape
    blocks = lax.axis_size("blk")
    devices = blocks * lax.axis_size("grp")
    place = lax.axis_index("blk") % QUAD
    everyone = range(blocks)
    f32 = jnp.float32
    scalars = jnp.stack(
        [jnp.exp(log_temp[0]), bias[0], jnp.where((place == 0) | (place == 3), 1.0, 0.0).astype(f32)]
    )

    def send(block, route):
        return lax.ppermute(block, "blk", route)

    beside = [(b, b ^ 1) for b in everyone]
    above = [(b, b ^ 2) for b in everyone]
    beyond = [(b, (b + QUAD if b % QUAD < 2 else b - QUAD) % blocks) for b in everyone]
    corner = [(b, b ^ 1) for b in everyone if b % QUAD in (1, 2)]
    middle_x = [(b, b ^ 1) for b in everyone if b % QUAD in (0, 3)]
    middle_y = [(b, b ^ 2) for b in everyone if b % QUAD in (0, 3)]

    txt_y = send(text, above)
    txt_x = send(text, beside)
    img_y = send(image, above)
    img_x = send(image, beside)

    tile = jax.ShapeDtypeStruct((rows, width), f32)
    unit = jax.ShapeDtypeStruct((rows, width), jnp.bfloat16)
    column = jax.ShapeDtypeStruct((rows, 128), f32)
    img_unit, txt_unit, img_inv, txt_inv, gx, gy, stats = call(
        own_kernel,
        [scalars, image, text],
        (unit, unit, column, column, tile, tile, jax.ShapeDtypeStruct((24, 128), f32)),
        rows,
        width,
        2,
    )

    txt_y, txt_x, gx, gy = tied(txt_y, txt_x, gx, gy)
    txt_z = send(txt_y, beyond)
    txt_m = send(txt_y, middle_x)
    gx, stats = visit(scalars, img_unit, txt_y, gx, stats)
    gx, stats = visit(scalars, img_unit, txt_x, gx, stats)
    img_y, img_x, gx = tied(img_y, img_x, gx)
    img_z = send(img_y, beyond)
    img_m = send(img_x, middle_y)
    (gy,) = visit(scalars, txt_unit, img_y, gy)
    txt_z, gy = tied(txt_z, gy)
    txt_c = send(txt_z, corner)
    (gy,) = visit(scalars, txt_unit, img_x, gy)
    gx, stats = visit(scalars, img_unit, txt_z, gx, stats)
    img_z, gx, gy = tied(img_z, gx, gy)
    img_c = send(img_z, corner)
    (gy,) = visit(scalars, txt_unit, img_z, gy)
    img_m, gx = tied(img_m, gx)
    grad_image, sums = visit(
        scalars, img_unit, txt_c, gx, stats, txt_m, (image, img_inv), devices
    )
    seen = lax.all_to_all(sums, ("blk", "grp"), 0, 0)
    pairs = jnp.float32(rows * rows * (2 * REACH + 1) * devices)
    statistics = jnp.sum(seen[:, 0, :3], axis=0) / pairs
    (grad_text,) = visit(scalars, txt_unit, img_c, gy, None, img_m, (text, txt_inv))
    return grad_image, grad_text, statistics


def solution(mesh):
    placed = P(("blk", "grp"), None)
    return jax.shard_map(
        on_device,
        mesh=mesh,
        in_specs=(placed, placed, P(), P()),
        out_specs=(placed, placed, P()),
        check_vma=False,
    )
```

```python
import functools

import jax
import jax.numpy as jnp
from jax import lax
from jax.experimental import pallas as pl
from jax.experimental.pallas import tpu as pltpu
from jax.sharding import PartitionSpec as P

REACH = 2
QUAD = 4
VMEM_LIMIT = 16 * 1024 * 1024
IN_VMEM = pl.BlockSpec(memory_space=pltpu.VMEM)
IN_SMEM = pl.BlockSpec(memory_space=pltpu.SMEM)


def unit_rows(raw):
    wide = raw.astype(jnp.float32)
    inverse = 1.0 / jnp.sqrt(jnp.sum(wide * wide, axis=1, keepdims=True) + 1e-06)
    return wide * inverse, inverse


def slopes(similar, temper, offset_bias, diagonal):
    logits = temper * similar + offset_bias
    tail = jnp.exp(-jnp.abs(logits))
    upper = jnp.where(logits >= 0, 1.0, tail) / (1.0 + tail)
    if not diagonal:
        return logits, tail, upper, logits
    lower = jnp.where(logits >= 0, tail, 1.0) / (1.0 + tail)
    same = lax.broadcasted_iota(jnp.int32, similar.shape, 0) == lax.broadcasted_iota(
        jnp.int32, similar.shape, 1
    )
    return logits, tail, jnp.where(same, -lower, upper), jnp.where(same, -logits, logits)


def fold(tile):
    rows, columns = tile.shape
    part = jnp.sum(tile.reshape(rows // 8, 8, columns), axis=0)
    return sum(part[:, c : c + 128] for c in range(0, columns, 128))


def tallies(margin, tail, slope, logits_part):
    pair_loss = jnp.maximum(margin, 0.0) + jnp.log1p(tail)
    return jnp.concatenate([fold(pair_loss), fold(slope * logits_part), fold(slope)], axis=0)


def across(left, right):
    return lax.dot_general(
        left, right, (((1,), (1,)), ((), ())), preferred_element_type=jnp.float32
    )


def own_kernel(scalars, image, text, img_unit, txt_unit, img_inv, txt_inv, gx, gy, stats):
    temper, offset_bias = scalars[0], scalars[1]
    x_wide, x_inv = unit_rows(image[...])
    y_wide, y_inv = unit_rows(text[...])
    x, y = x_wide.astype(jnp.bfloat16), y_wide.astype(jnp.bfloat16)
    img_unit[...] = x
    txt_unit[...] = y
    img_inv[...] = jnp.broadcast_to(x_inv, img_inv.shape)
    txt_inv[...] = jnp.broadcast_to(y_inv, txt_inv.shape)
    similar = across(x, y)
    _, tail, slope, margin = slopes(similar, temper, offset_bias, True)
    stats[...] = tallies(margin, tail, slope, temper * similar)
    scaled = (temper * slope).astype(jnp.bfloat16)
    gx[...] = jnp.dot(scaled, y, preferred_element_type=jnp.float32)
    _, _, slope, _ = slopes(across(y, x), temper, offset_bias, True)
    scaled = (temper * slope).astype(jnp.bfloat16)
    gy[...] = jnp.dot(scaled, x, preferred_element_type=jnp.float32)


def widened(ref):
    return ref[...].astype(jnp.float32)


def rounded_unit(raw):
    return unit_rows(raw)[0].astype(jnp.bfloat16)


def meet(scalars, own, unit, counted=False):
    temper, offset_bias = scalars[0], scalars[1]
    similar = across(own, unit)
    logits, tail, slope, _ = slopes(similar, temper, offset_bias, False)
    scaled = (temper * slope).astype(jnp.bfloat16)
    grad = jnp.dot(scaled, unit, preferred_element_type=jnp.float32)
    tally = tallies(logits, tail, slope, temper * similar) if counted else None
    return grad, tally


def finished(grad, raw, inverse):
    inv = inverse[:, :1]
    wide = widened(raw) * inv
    return inv * (grad - wide * jnp.sum(wide * grad, axis=1, keepdims=True))


def text_pair_kernel(scalars, own, first, second, gx, stats, gx_out, stats_out, unit_out):
    unit = rounded_unit(widened(first))
    unit_out[...] = unit
    grad_a, tally_a = meet(scalars, own[...], unit, True)
    grad_b, tally_b = meet(scalars, own[...], rounded_unit(widened(second)), True)
    gx_out[...] = gx[...] + grad_a + grad_b
    stats_out[...] = stats[...] + tally_a + tally_b


def image_pair_kernel(scalars, own, first, second, gy, gy_out, part, unit_out):
    part[...] = second[: part.shape[0]]
    unit = rounded_unit(widened(second))
    unit_out[...] = unit
    grad_a, _ = meet(scalars, own[...], rounded_unit(widened(first)))
    grad_b, _ = meet(scalars, own[...], unit)
    gy_out[...] = gy[...] + grad_a + grad_b


def text_far_kernel(scalars, own, far, near_image, near_text, gx, stats, gx_out, sums_out):
    temper, offset_bias = scalars[0], scalars[1]
    wide = unit_rows(widened(far))[0]
    grad, tally = meet(scalars, own[...], wide.astype(jnp.bfloat16), True)
    gx_out[...] = gx[...] + grad
    partner = jnp.where(scalars[2] > 0.5, widened(near_text), wide).astype(jnp.bfloat16)
    similar = across(near_image[...], partner)
    logits, tail, slope, _ = slopes(similar, temper, offset_bias, False)
    tally = stats[...] + tally + tallies(logits, tail, slope, temper * similar)
    lane = lax.broadcasted_iota(jnp.int32, (8, 128), 1)
    sums = [jnp.sum(tally[8 * i : 8 * i + 8]) for i in range(3)]
    row = jnp.where(lane == 0, sums[0], jnp.where(lane == 1, sums[1], sums[2]))
    sums_out[...] = jnp.broadcast_to(row[None], sums_out.shape)


def image_far_kernel(scalars, own, far, upper, middle, gy, gy_out):
    grad_a, _ = meet(scalars, own[...], rounded_unit(widened(far)))
    block = jnp.where(scalars[2] > 0.5, widened(upper), widened(middle.at[: upper.shape[0]]))
    grad_b, _ = meet(scalars, own[...], rounded_unit(block))
    gy_out[...] = gy[...] + grad_a + grad_b


def pick_kernel(scalars, outer, inner, out):
    out[...] = jnp.where(scalars[2] > 0.5, widened(outer), widened(inner)).astype(out.dtype)


def last_text_kernel(scalars, own, block, acc, raw, inverse, out):
    grad, _ = meet(scalars, own[...], rounded_unit(widened(block)))
    out[...] = finished(acc[...] + grad, raw, inverse)


def last_image_kernel(scalars, own, lower, middle, acc, raw, inverse, out):
    rest = widened(middle.at[middle.shape[0] - lower.shape[0] :])
    block = jnp.where(scalars[2] > 0.5, widened(lower), rest)
    grad, _ = meet(scalars, own[...], rounded_unit(block))
    out[...] = finished(acc[...] + grad, raw, inverse)


def tied(*values):
    return lax.optimization_barrier(values)


def cost(rows, width, tiles):
    return pl.CostEstimate(
        flops=4 * tiles * rows * rows * width,
        bytes_accessed=12 * tiles * rows * width,
        transcendentals=tiles * rows * rows,
    )


def call(kernel, operands, shapes, rows, width, tiles):
    return pl.pallas_call(
        kernel,
        out_shape=shapes,
        in_specs=[IN_SMEM] + [IN_VMEM] * (len(operands) - 1),
        out_specs=tuple(IN_VMEM for _ in shapes),
        compiler_params=pltpu.CompilerParams(vmem_limit_bytes=VMEM_LIMIT),
        cost_estimate=cost(rows, width, tiles),
    )(*operands)


def on_device(image, text, log_temp, bias):
    rows, width = image.shape
    half = rows // 2
    blocks = lax.axis_size("blk")
    devices = blocks * lax.axis_size("grp")
    place = lax.axis_index("blk") % QUAD
    everyone = range(blocks)
    f32 = jnp.float32
    scalars = jnp.stack(
        [jnp.exp(log_temp[0]), bias[0], jnp.where((place == 0) | (place == 3), 1.0, 0.0).astype(f32)]
    )

    def send(block, route):
        return lax.ppermute(block, "blk", route)

    beside = [(b, b ^ 1) for b in everyone]
    above = [(b, b ^ 2) for b in everyone]
    beyond = [(b, (b + QUAD if b % QUAD < 2 else b - QUAD) % blocks) for b in everyone]
    corner = [(b, b ^ 1) for b in everyone if b % QUAD in (1, 2)]
    turn = [(b, (b + 2 if b % QUAD == 2 else b - 2) % blocks) for b in everyone if b % QUAD in (1, 2)]
    middle = [(b, b ^ 1) for b in everyone if b % QUAD in (0, 3)]
    mixed = [(b, b ^ (1 if b % QUAD in (1, 2) else 2)) for b in everyone]

    tile = jax.ShapeDtypeStruct((rows, width), f32)
    unit = jax.ShapeDtypeStruct((rows, width), jnp.bfloat16)
    part = jax.ShapeDtypeStruct((half, width), jnp.bfloat16)
    column = jax.ShapeDtypeStruct((rows, 128), f32)
    tally = jax.ShapeDtypeStruct((24, 128), f32)
    spread = jax.ShapeDtypeStruct((devices, 8, 128), f32)

    def run(kernel, tiles, operands, *shapes):
        return call(kernel, [scalars, *operands], shapes, rows, width, tiles)

    txt_y = send(text, above)
    txt_x = send(text, beside)
    img_y = send(image, above)
    img_x = send(image, beside)
    img_unit, txt_unit, img_inv, txt_inv, gx, gy, stats = run(
        own_kernel, 2, [image, text], unit, unit, column, column, tile, tile, tally
    )

    txt_y, gx, gy = tied(txt_y, gx, gy)
    txt_z = send(txt_y, beyond)
    gx, stats, unit_y = run(
        text_pair_kernel, 2, [img_unit, txt_y, txt_x, gx, stats], tile, tally, unit
    )
    img_y, img_x, gx = tied(img_y, img_x, gx)
    img_z = send(img_y, beyond)
    (txt_v,) = run(pick_kernel, 1, [txt_x, txt_z], unit)
    txt_w = send(txt_v, mixed)
    txt_v, gy, img_y = tied(txt_v, gy, img_y)
    img_m = send(img_y, middle)
    gy, img_h, unit_x = run(
        image_pair_kernel, 2, [txt_unit, img_y, img_x, gy], tile, part, unit
    )
    img_t = send(img_h, turn)
    gx, sums = run(
        text_far_kernel, 2, [img_unit, txt_z, unit_x, unit_y, gx, stats], tile, spread
    )
    img_z, gx, gy = tied(img_z, gx, gy)
    img_c = send(img_z[half:], corner)
    (gy,) = run(image_far_kernel, 2, [txt_unit, img_z, img_t, img_m, gy], tile)
    img_m, gx, gy = tied(img_m, gx, gy)
    sums, txt_w = tied(sums, txt_w)
    seen = lax.all_to_all(sums, ("blk", "grp"), 0, 0)
    pairs = jnp.float32(rows * rows * (2 * REACH + 1) * devices)
    statistics = jnp.sum(seen[:, 0, :3], axis=0) / pairs
    (grad_image,) = run(last_text_kernel, 1, [img_unit, txt_w, gx, image, img_inv], tile)
    (grad_text,) = run(
        last_image_kernel, 1, [txt_unit, img_c, img_m, gy, text, txt_inv], tile
    )
    return grad_image, grad_text, statistics


def solution(mesh):
    placed = P(("blk", "grp"), None)
    return jax.shard_map(
        on_device,
        mesh=mesh,
        in_specs=(placed, placed, P(), P()),
        out_specs=(placed, placed, P()),
        check_vma=False,
    )
```

```python
import functools

import jax
import jax.numpy as jnp
from jax import lax
from jax.experimental import pallas as pl
from jax.experimental.pallas import tpu as pltpu
from jax.sharding import PartitionSpec as P

REACH = 2
QUAD = 4
VMEM_LIMIT = 16 * 1024 * 1024
IN_VMEM = pl.BlockSpec(memory_space=pltpu.VMEM)
IN_SMEM = pl.BlockSpec(memory_space=pltpu.SMEM)


def unit_rows(raw):
    wide = raw.astype(jnp.float32)
    inverse = 1.0 / jnp.sqrt(jnp.sum(wide * wide, axis=1, keepdims=True) + 1e-06)
    return wide * inverse, inverse


def slopes(similar, temper, offset_bias, diagonal):
    logits = temper * similar + offset_bias
    tail = jnp.exp(-jnp.abs(logits))
    upper = jnp.where(logits >= 0, 1.0, tail) / (1.0 + tail)
    if not diagonal:
        return logits, tail, upper, logits
    lower = jnp.where(logits >= 0, tail, 1.0) / (1.0 + tail)
    same = lax.broadcasted_iota(jnp.int32, similar.shape, 0) == lax.broadcasted_iota(
        jnp.int32, similar.shape, 1
    )
    return logits, tail, jnp.where(same, -lower, upper), jnp.where(same, -logits, logits)


def fold(tile):
    rows, columns = tile.shape
    part = jnp.sum(tile.reshape(rows // 8, 8, columns), axis=0)
    return sum(part[:, c : c + 128] for c in range(0, columns, 128))


def tallies(margin, tail, slope, logits_part):
    pair_loss = jnp.maximum(margin, 0.0) + jnp.log1p(tail)
    return jnp.concatenate([fold(pair_loss), fold(slope * logits_part), fold(slope)], axis=0)


def across(left, right):
    return lax.dot_general(
        left, right, (((1,), (1,)), ((), ())), preferred_element_type=jnp.float32
    )


def own_kernel(scalars, image, text, img_unit, txt_unit, img_inv, txt_inv, gx, gy, stats):
    temper, offset_bias = scalars[0], scalars[1]
    x_wide, x_inv = unit_rows(image[...])
    y_wide, y_inv = unit_rows(text[...])
    x, y = x_wide.astype(jnp.bfloat16), y_wide.astype(jnp.bfloat16)
    img_unit[...] = x
    txt_unit[...] = y
    img_inv[...] = jnp.broadcast_to(x_inv, img_inv.shape)
    txt_inv[...] = jnp.broadcast_to(y_inv, txt_inv.shape)
    similar = across(x, y)
    _, tail, slope, margin = slopes(similar, temper, offset_bias, True)
    stats[...] = tallies(margin, tail, slope, temper * similar)
    scaled = (temper * slope).astype(jnp.bfloat16)
    gx[...] = jnp.dot(scaled, y, preferred_element_type=jnp.float32)
    _, _, slope, _ = slopes(across(y, x), temper, offset_bias, True)
    scaled = (temper * slope).astype(jnp.bfloat16)
    gy[...] = jnp.dot(scaled, x, preferred_element_type=jnp.float32)


def widened(ref):
    return ref[...].astype(jnp.float32)


def rounded_unit(raw):
    return unit_rows(raw)[0].astype(jnp.bfloat16)


def meet(scalars, own, unit, counted=False):
    temper, offset_bias = scalars[0], scalars[1]
    similar = across(own, unit)
    logits, tail, slope, _ = slopes(similar, temper, offset_bias, False)
    scaled = (temper * slope).astype(jnp.bfloat16)
    grad = jnp.dot(scaled, unit, preferred_element_type=jnp.float32)
    tally = tallies(logits, tail, slope, temper * similar) if counted else None
    return grad, tally


def finish(out, grad, raw, inverse):
    inv = inverse[...]
    spans = [slice(c, c + 128) for c in range(0, raw.shape[1], 128)]
    dot = sum(widened(raw.at[:, s]) * grad[:, s] for s in spans)
    pull = jnp.sum(dot, axis=1, keepdims=True) * (inv * inv * inv)
    for s in spans:
        out[:, s] = inv * grad[:, s] - widened(raw.at[:, s]) * pull


def text_pair_kernel(scalars, own, first, second, gx, stats, gx_out, stats_out, unit_out):
    unit = rounded_unit(widened(first))
    unit_out[...] = unit
    grad_a, tally_a = meet(scalars, own[...], unit, True)
    grad_b, tally_b = meet(scalars, own[...], rounded_unit(widened(second)), True)
    gx_out[...] = gx[...] + grad_a + grad_b
    stats_out[...] = stats[...] + tally_a + tally_b


def image_pair_kernel(scalars, own, first, second, gy, gy_out, unit_out):
    unit = rounded_unit(widened(second))
    unit_out[...] = unit
    grad_a, _ = meet(scalars, own[...], rounded_unit(widened(first)))
    grad_b, _ = meet(scalars, own[...], unit)
    gy_out[...] = gy[...] + grad_a + grad_b


def text_far_kernel(scalars, own, far, near_image, near_text, gx, stats, gx_out, sums_out):
    temper, offset_bias = scalars[0], scalars[1]
    wide = unit_rows(widened(far))[0]
    grad, tally = meet(scalars, own[...], wide.astype(jnp.bfloat16), True)
    gx_out[...] = gx[...] + grad
    partner = jnp.where(scalars[2] > 0.5, widened(near_text), wide).astype(jnp.bfloat16)
    similar = across(near_image[...], partner)
    logits, tail, slope, _ = slopes(similar, temper, offset_bias, False)
    tally = stats[...] + tally + tallies(logits, tail, slope, temper * similar)
    lane = lax.broadcasted_iota(jnp.int32, (8, 128), 1)
    sums = [jnp.sum(tally[8 * i : 8 * i + 8]) for i in range(3)]
    row = jnp.where(lane == 0, sums[0], jnp.where(lane == 1, sums[1], sums[2]))
    sums_out[...] = jnp.broadcast_to((row * scalars[3])[None], sums_out.shape)


def chosen(scalars, outer, inner):
    return jnp.where(scalars[2] > 0.5, widened(outer), widened(inner)).astype(outer.dtype)


def pick_kernel(scalars, outer, inner, whole, out, part):
    out[...] = chosen(scalars, outer, inner)
    part[...] = whole[: part.shape[0]]


def pick_half_kernel(scalars, outer, inner, out):
    half = out.shape[0]
    out[...] = chosen(scalars, outer.at[half:], inner.at[half:])


def last_kernel(scalars, own, *refs):
    *pieces, acc, raw, inverse, out = refs
    grad = acc[...]
    for piece in pieces:
        grad += meet(scalars, own[...], rounded_unit(widened(piece)))[0]
    finish(out, grad, raw, inverse)


def tied(*values):
    return lax.optimization_barrier(values)


def cost(rows, width, tiles):
    return pl.CostEstimate(
        flops=4 * tiles * rows * rows * width,
        bytes_accessed=12 * tiles * rows * width,
        transcendentals=tiles * rows * rows,
    )


def call(kernel, operands, shapes, rows, width, tiles):
    return pl.pallas_call(
        kernel,
        out_shape=shapes,
        in_specs=[IN_SMEM] + [IN_VMEM] * (len(operands) - 1),
        out_specs=tuple(IN_VMEM for _ in shapes),
        compiler_params=pltpu.CompilerParams(vmem_limit_bytes=VMEM_LIMIT),
        cost_estimate=cost(rows, width, tiles),
    )(*operands)


def on_device(image, text, log_temp, bias):
    rows, width = image.shape
    half = rows // 2
    blocks = lax.axis_size("blk")
    devices = blocks * lax.axis_size("grp")
    place = lax.axis_index("blk") % QUAD
    everyone = range(blocks)
    f32 = jnp.float32
    share = 1.0 / (rows * rows * (2 * REACH + 1) * devices)
    outer = jnp.where((place == 0) | (place == 3), 1.0, 0.0).astype(f32)
    scalars = jnp.stack([jnp.exp(log_temp[0]), bias[0], outer, jnp.full((), share, f32)])

    def send(block, route):
        return lax.ppermute(block, "blk", route)

    beside = [(b, b ^ 1) for b in everyone]
    above = [(b, b ^ 2) for b in everyone]
    beyond = [(b, (b + QUAD if b % QUAD < 2 else b - QUAD) % blocks) for b in everyone]
    def turned(b):
        step = {0: 2, 1: -2, 2: 2, 3: -2}[b % QUAD]
        return (b + step) % blocks

    turn = [(b, turned(b)) for b in everyone]

    tile = jax.ShapeDtypeStruct((rows, width), f32)
    unit = jax.ShapeDtypeStruct((rows, width), jnp.bfloat16)
    part = jax.ShapeDtypeStruct((half, width), jnp.bfloat16)
    column = jax.ShapeDtypeStruct((rows, 128), f32)
    tally = jax.ShapeDtypeStruct((24, 128), f32)
    spread = jax.ShapeDtypeStruct((devices, 8, 128), f32)

    def run(kernel, tiles, operands, *shapes):
        return call(kernel, [scalars, *operands], shapes, rows, width, tiles)

    txt_y = send(text, above)
    txt_x = send(text, beside)
    img_y = send(image, above)
    img_x = send(image, beside)
    img_unit, txt_unit, img_inv, txt_inv, gx, gy, stats = run(
        own_kernel, 2, [image, text], unit, unit, column, column, tile, tile, tally
    )

    txt_y, gx, gy = tied(txt_y, gx, gy)
    txt_z = send(txt_y, beyond)
    gx, stats, unit_y = run(
        text_pair_kernel, 2, [img_unit, txt_y, txt_x, gx, stats], tile, tally, unit
    )
    img_y, img_x, gx = tied(img_y, img_x, gx)
    img_z = send(img_y, beyond)
    txt_z, img_x, img_y = tied(txt_z, img_x, img_y)
    txt_v, img_h = run(pick_kernel, 1, [txt_y, txt_z, img_x], unit, part)
    txt_w = send(txt_v, beside)
    img_k = send(img_h, turn)
    txt_v, gy = tied(txt_v, gy)
    gy, unit_x = run(image_pair_kernel, 2, [txt_unit, img_y, img_x, gy], tile, unit)
    gx, sums = run(
        text_far_kernel, 2, [img_unit, txt_z, unit_x, unit_y, gx, stats], tile, spread
    )
    img_z, gx, gy = tied(img_z, gx, gy)
    (img_v,) = run(pick_half_kernel, 1, [img_y, img_z], part)
    img_w = send(img_v, beside)
    sums, txt_w = tied(sums, txt_w)
    seen = lax.all_to_all(sums, ("blk", "grp"), 0, 0)
    statistics = jnp.sum(seen[:, 0, :3], axis=0)
    (grad_image,) = run(last_kernel, 1, [img_unit, txt_w, gx, image, img_inv], tile)
    gy, grad_image = tied(gy, grad_image)
    (grad_text,) = run(last_kernel, 1, [txt_unit, img_z, img_k, img_w, gy, text, txt_inv], tile)
    return grad_image, grad_text, statistics


def solution(mesh):
    placed = P(("blk", "grp"), None)
    return jax.shard_map(
        on_device,
        mesh=mesh,
        in_specs=(placed, placed, P(), P()),
        out_specs=(placed, placed, P()),
        check_vma=False,
    )
```

```python
import functools

import jax
import jax.numpy as jnp
from jax import lax
from jax.experimental import pallas as pl
from jax.experimental.pallas import tpu as pltpu
from jax.sharding import PartitionSpec as P

REACH = 2
QUAD = 4
VMEM_LIMIT = 16 * 1024 * 1024
IN_VMEM = pl.BlockSpec(memory_space=pltpu.VMEM)
IN_SMEM = pl.BlockSpec(memory_space=pltpu.SMEM)


def unit_rows(raw):
    wide = raw.astype(jnp.float32)
    inverse = 1.0 / jnp.sqrt(jnp.sum(wide * wide, axis=1, keepdims=True) + 1e-06)
    return wide * inverse, inverse


def slopes(similar, temper, offset_bias, diagonal):
    logits = temper * similar + offset_bias
    tail = jnp.exp(-jnp.abs(logits))
    upper = jnp.where(logits >= 0, 1.0, tail) / (1.0 + tail)
    if not diagonal:
        return logits, tail, upper, logits
    lower = jnp.where(logits >= 0, tail, 1.0) / (1.0 + tail)
    same = lax.broadcasted_iota(jnp.int32, similar.shape, 0) == lax.broadcasted_iota(
        jnp.int32, similar.shape, 1
    )
    return logits, tail, jnp.where(same, -lower, upper), jnp.where(same, -logits, logits)


def fold(tile):
    rows, columns = tile.shape
    part = jnp.sum(tile.reshape(rows // 8, 8, columns), axis=0)
    return sum(part[:, c : c + 128] for c in range(0, columns, 128))


def tallies(margin, tail, slope, logits_part):
    pair_loss = jnp.maximum(margin, 0.0) + jnp.log1p(tail)
    return jnp.concatenate([fold(pair_loss), fold(slope * logits_part), fold(slope)], axis=0)


def across(left, right):
    return lax.dot_general(
        left, right, (((1,), (1,)), ((), ())), preferred_element_type=jnp.float32
    )


def own_kernel(scalars, image, text, img_unit, txt_unit, img_inv, txt_inv, gx, gy, stats):
    temper, offset_bias = scalars[0], scalars[1]
    x_wide, x_inv = unit_rows(image[...])
    y_wide, y_inv = unit_rows(text[...])
    x, y = x_wide.astype(jnp.bfloat16), y_wide.astype(jnp.bfloat16)
    img_unit[...] = x
    txt_unit[...] = y
    img_inv[...] = jnp.broadcast_to(x_inv, img_inv.shape)
    txt_inv[...] = jnp.broadcast_to(y_inv, txt_inv.shape)
    similar = across(x, y)
    _, tail, slope, margin = slopes(similar, temper, offset_bias, True)
    stats[...] = tallies(margin, tail, slope, temper * similar)
    scaled = (temper * slope).astype(jnp.bfloat16)
    gx[...] = jnp.dot(scaled, y, preferred_element_type=jnp.float32)
    _, _, slope, _ = slopes(across(y, x), temper, offset_bias, True)
    scaled = (temper * slope).astype(jnp.bfloat16)
    gy[...] = jnp.dot(scaled, x, preferred_element_type=jnp.float32)


def widened(ref):
    return ref[...].astype(jnp.float32)


def rounded_unit(raw):
    return unit_rows(raw)[0].astype(jnp.bfloat16)


def meet(scalars, own, unit, counted=False):
    temper, offset_bias = scalars[0], scalars[1]
    similar = across(own, unit)
    logits, tail, slope, _ = slopes(similar, temper, offset_bias, False)
    scaled = (temper * slope).astype(jnp.bfloat16)
    grad = jnp.dot(scaled, unit, preferred_element_type=jnp.float32)
    tally = tallies(logits, tail, slope, temper * similar) if counted else None
    return grad, tally


def finish(out, grad, raw, inverse):
    inv = inverse[...]
    spans = [slice(c, c + 128) for c in range(0, raw.shape[1], 128)]
    dot = sum(widened(raw.at[:, s]) * grad[:, s] for s in spans)
    pull = jnp.sum(dot, axis=1, keepdims=True) * (inv * inv * inv)
    for s in spans:
        out[:, s] = inv * grad[:, s] - widened(raw.at[:, s]) * pull


def text_pair_kernel(scalars, own, first, second, gx, stats, gx_out, stats_out, unit_out):
    unit = rounded_unit(widened(first))
    unit_out[...] = unit
    grad_a, tally_a = meet(scalars, own[...], unit, True)
    grad_b, tally_b = meet(scalars, own[...], rounded_unit(widened(second)), True)
    gx_out[...] = gx[...] + grad_a + grad_b
    stats_out[...] = stats[...] + tally_a + tally_b


def image_pair_kernel(scalars, own, first, second, gy, gy_out, unit_out):
    unit = rounded_unit(widened(second))
    unit_out[...] = unit
    grad_a, _ = meet(scalars, own[...], rounded_unit(widened(first)))
    grad_b, _ = meet(scalars, own[...], unit)
    gy_out[...] = gy[...] + grad_a + grad_b


def text_far_kernel(scalars, own, far, near_image, near_text, gx, stats, gx_out, sums_out):
    temper, offset_bias = scalars[0], scalars[1]
    wide = unit_rows(widened(far))[0]
    grad, tally = meet(scalars, own[...], wide.astype(jnp.bfloat16), True)
    gx_out[...] = gx[...] + grad
    partner = jnp.where(scalars[2] > 0.5, widened(near_text), wide).astype(jnp.bfloat16)
    similar = across(near_image[...], partner)
    logits, tail, slope, _ = slopes(similar, temper, offset_bias, False)
    tally = stats[...] + tally + tallies(logits, tail, slope, temper * similar)
    lane = lax.broadcasted_iota(jnp.int32, (8, 128), 1)
    sums = [jnp.sum(tally[8 * i : 8 * i + 8]) for i in range(3)]
    row = jnp.where(lane == 0, sums[0], jnp.where(lane == 1, sums[1], sums[2]))
    sums_out[...] = jnp.broadcast_to((row * scalars[3])[None], sums_out.shape)


def image_far_kernel(scalars, own, far, out):
    out[...] = meet(scalars, own[...], rounded_unit(widened(far)))[0]


def chosen(scalars, outer, inner):
    return jnp.where(scalars[2] > 0.5, widened(outer), widened(inner)).astype(outer.dtype)


def pick_kernel(scalars, outer, inner, whole, out, part):
    out[...] = chosen(scalars, outer, inner)
    part[...] = whole[: part.shape[0]]


def pick_half_kernel(scalars, outer, inner, out):
    half = out.shape[0]
    out[...] = chosen(scalars, outer.at[half:], inner.at[half:])


def last_kernel(count, scalars, own, *refs):
    pieces, (*sums, raw, inverse, out) = refs[:count], refs[count:]
    grad = sum(held[...] for held in sums)
    for piece in pieces:
        grad += meet(scalars, own[...], rounded_unit(widened(piece)))[0]
    finish(out, grad, raw, inverse)


def tied(*values):
    return lax.optimization_barrier(values)


def cost(rows, width, tiles):
    return pl.CostEstimate(
        flops=4 * tiles * rows * rows * width,
        bytes_accessed=12 * tiles * rows * width,
        transcendentals=tiles * rows * rows,
    )


def call(kernel, operands, shapes, rows, width, tiles):
    return pl.pallas_call(
        kernel,
        out_shape=shapes,
        in_specs=[IN_SMEM] + [IN_VMEM] * (len(operands) - 1),
        out_specs=tuple(IN_VMEM for _ in shapes),
        compiler_params=pltpu.CompilerParams(vmem_limit_bytes=VMEM_LIMIT),
        cost_estimate=cost(rows, width, tiles),
    )(*operands)


def on_device(image, text, log_temp, bias):
    rows, width = image.shape
    half = rows // 2
    blocks = lax.axis_size("blk")
    devices = blocks * lax.axis_size("grp")
    place = lax.axis_index("blk") % QUAD
    everyone = range(blocks)
    f32 = jnp.float32
    share = 1.0 / (rows * rows * (2 * REACH + 1) * devices)
    outer = jnp.where((place == 0) | (place == 3), 1.0, 0.0).astype(f32)
    scalars = jnp.stack([jnp.exp(log_temp[0]), bias[0], outer, jnp.full((), share, f32)])

    def send(block, route):
        return lax.ppermute(block, "blk", route)

    beside = [(b, b ^ 1) for b in everyone]
    above = [(b, b ^ 2) for b in everyone]
    beyond = [(b, (b + QUAD if b % QUAD < 2 else b - QUAD) % blocks) for b in everyone]
    def turned(b):
        step = {0: 2, 1: -2, 2: 2, 3: -2}[b % QUAD]
        return (b + step) % blocks

    turn = [(b, turned(b)) for b in everyone]

    tile = jax.ShapeDtypeStruct((rows, width), f32)
    unit = jax.ShapeDtypeStruct((rows, width), jnp.bfloat16)
    part = jax.ShapeDtypeStruct((half, width), jnp.bfloat16)
    column = jax.ShapeDtypeStruct((rows, 128), f32)
    tally = jax.ShapeDtypeStruct((24, 128), f32)
    spread = jax.ShapeDtypeStruct((devices, 8, 128), f32)

    def run(kernel, tiles, operands, *shapes):
        return call(kernel, [scalars, *operands], shapes, rows, width, tiles)

    txt_y = send(text, above)
    txt_x = send(text, beside)
    img_y = send(image, above)
    img_x = send(image, beside)
    img_unit, txt_unit, img_inv, txt_inv, gx, gy, stats = run(
        own_kernel, 2, [image, text], unit, unit, column, column, tile, tile, tally
    )

    txt_y, gx, gy = tied(txt_y, gx, gy)
    txt_z = send(txt_y, beyond)
    gx, stats, unit_y = run(
        text_pair_kernel, 2, [img_unit, txt_y, txt_x, gx, stats], tile, tally, unit
    )
    img_y, img_x, gx = tied(img_y, img_x, gx)
    img_z = send(img_y, beyond)
    txt_z, img_x, img_y = tied(txt_z, img_x, img_y)
    txt_v, img_h = run(pick_kernel, 1, [txt_y, txt_z, img_x], unit, part)
    txt_w = send(txt_v, beside)
    img_k = send(img_h, turn)
    txt_v, gy = tied(txt_v, gy)
    gy, unit_x = run(image_pair_kernel, 2, [txt_unit, img_y, img_x, gy], tile, unit)
    gx, sums = run(
        text_far_kernel, 2, [img_unit, txt_z, unit_x, unit_y, gx, stats], tile, spread
    )
    img_z, gx, gy = tied(img_z, gx, gy)
    (img_v,) = run(pick_half_kernel, 1, [img_y, img_z], part)
    img_w = send(img_v, beside)
    sums, txt_w = tied(sums, txt_w)
    seen = lax.all_to_all(sums, ("blk", "grp"), 0, 0)
    statistics = jnp.sum(seen[:, 0, :3], axis=0)
    (far,) = run(image_far_kernel, 1, [txt_unit, img_z], tile)
    far, gx = tied(far, gx)
    (grad_image,) = run(
        functools.partial(last_kernel, 1), 1, [img_unit, txt_w, gx, image, img_inv], tile
    )
    gy, grad_image = tied(gy, grad_image)
    (grad_text,) = run(
        functools.partial(last_kernel, 2),
        1,
        [txt_unit, img_k, img_w, gy, far, text, txt_inv],
        tile,
    )
    return grad_image, grad_text, statistics


def solution(mesh):
    placed = P(("blk", "grp"), None)
    return jax.shard_map(
        on_device,
        mesh=mesh,
        in_specs=(placed, placed, P(), P()),
        out_specs=(placed, placed, P()),
        check_vma=False,
    )
```

```python
import functools

import jax
import jax.numpy as jnp
from jax import lax
from jax.experimental import pallas as pl
from jax.experimental.pallas import tpu as pltpu
from jax.sharding import PartitionSpec as P

REACH = 2
QUAD = 4
VMEM_LIMIT = 16 * 1024 * 1024
IN_VMEM = pl.BlockSpec(memory_space=pltpu.VMEM)
IN_SMEM = pl.BlockSpec(memory_space=pltpu.SMEM)


def unit_rows(raw):
    wide = raw.astype(jnp.float32)
    inverse = 1.0 / jnp.sqrt(jnp.sum(wide * wide, axis=1, keepdims=True) + 1e-06)
    return wide * inverse, inverse


def slopes(similar, temper, offset_bias, diagonal):
    logits = temper * similar + offset_bias
    tail = jnp.exp(-jnp.abs(logits))
    upper = jnp.where(logits >= 0, 1.0, tail) / (1.0 + tail)
    if not diagonal:
        return logits, tail, upper, logits
    lower = jnp.where(logits >= 0, tail, 1.0) / (1.0 + tail)
    same = lax.broadcasted_iota(jnp.int32, similar.shape, 0) == lax.broadcasted_iota(
        jnp.int32, similar.shape, 1
    )
    return logits, tail, jnp.where(same, -lower, upper), jnp.where(same, -logits, logits)


def fold(tile):
    rows, columns = tile.shape
    part = jnp.sum(tile.reshape(rows // 8, 8, columns), axis=0)
    return sum(part[:, c : c + 128] for c in range(0, columns, 128))


def tallies(margin, tail, slope, logits_part):
    pair_loss = jnp.maximum(margin, 0.0) + jnp.log1p(tail)
    return jnp.concatenate([fold(pair_loss), fold(slope * logits_part), fold(slope)], axis=0)


def across(left, right):
    return lax.dot_general(
        left, right, (((1,), (1,)), ((), ())), preferred_element_type=jnp.float32
    )


def own_kernel(scalars, image, text, img_unit, txt_unit, img_inv, txt_inv, gx, gy, stats):
    temper, offset_bias = scalars[0], scalars[1]
    x_wide, x_inv = unit_rows(image[...])
    y_wide, y_inv = unit_rows(text[...])
    x, y = x_wide.astype(jnp.bfloat16), y_wide.astype(jnp.bfloat16)
    img_unit[...] = x
    txt_unit[...] = y
    img_inv[...] = jnp.broadcast_to(x_inv, img_inv.shape)
    txt_inv[...] = jnp.broadcast_to(y_inv, txt_inv.shape)
    similar = across(x, y)
    _, tail, slope, margin = slopes(similar, temper, offset_bias, True)
    stats[...] = tallies(margin, tail, slope, temper * similar)
    scaled = (temper * slope).astype(jnp.bfloat16)
    gx[...] = jnp.dot(scaled, y, preferred_element_type=jnp.float32)
    _, _, slope, _ = slopes(across(y, x), temper, offset_bias, True)
    scaled = (temper * slope).astype(jnp.bfloat16)
    gy[...] = jnp.dot(scaled, x, preferred_element_type=jnp.float32)


def widened(ref):
    return ref[...].astype(jnp.float32)


def rounded_unit(raw):
    return unit_rows(raw)[0].astype(jnp.bfloat16)


def meet(scalars, own, unit, counted=False):
    temper, offset_bias = scalars[0], scalars[1]
    similar = across(own, unit)
    logits, tail, slope, _ = slopes(similar, temper, offset_bias, False)
    scaled = (temper * slope).astype(jnp.bfloat16)
    grad = jnp.dot(scaled, unit, preferred_element_type=jnp.float32)
    tally = tallies(logits, tail, slope, temper * similar) if counted else None
    return grad, tally


def finish(out, grad, raw, inverse):
    inv = inverse[...]
    spans = [slice(c, c + 128) for c in range(0, raw.shape[1], 128)]
    dot = sum(widened(raw.at[:, s]) * grad[:, s] for s in spans)
    pull = jnp.sum(dot, axis=1, keepdims=True) * (inv * inv * inv)
    for s in spans:
        out[:, s] = inv * grad[:, s] - widened(raw.at[:, s]) * pull


def text_pair_kernel(scalars, own, first, second, gx, stats, gx_out, stats_out, unit_out):
    unit = rounded_unit(widened(first))
    unit_out[...] = unit
    grad_a, tally_a = meet(scalars, own[...], unit, True)
    grad_b, tally_b = meet(scalars, own[...], rounded_unit(widened(second)), True)
    gx_out[...] = gx[...] + grad_a + grad_b
    stats_out[...] = stats[...] + tally_a + tally_b


def image_pair_kernel(scalars, own, first, second, gy, gy_out, unit_out):
    unit = rounded_unit(widened(second))
    unit_out[...] = unit
    grad_a, _ = meet(scalars, own[...], rounded_unit(widened(first)))
    grad_b, _ = meet(scalars, own[...], unit)
    gy_out[...] = gy[...] + grad_a + grad_b


def text_far_kernel(scalars, own, far, near_image, near_text, gx, stats, gx_out, sums_out):
    temper, offset_bias = scalars[0], scalars[1]
    wide = unit_rows(widened(far))[0]
    grad, tally = meet(scalars, own[...], wide.astype(jnp.bfloat16), True)
    gx_out[...] = gx[...] + grad
    partner = jnp.where(scalars[2] > 0.5, widened(near_text), wide).astype(jnp.bfloat16)
    similar = across(near_image[...], partner)
    logits, tail, slope, _ = slopes(similar, temper, offset_bias, False)
    tally = stats[...] + tally + tallies(logits, tail, slope, temper * similar)
    lane = lax.broadcasted_iota(jnp.int32, (8, 128), 1)
    sums = [jnp.sum(tally[8 * i : 8 * i + 8]) for i in range(3)]
    row = jnp.where(lane == 0, sums[0], jnp.where(lane == 1, sums[1], sums[2]))
    sums_out[...] = jnp.broadcast_to((row * scalars[3])[:4][None], sums_out.shape)


def image_far_kernel(scalars, own, far, out):
    out[...] = meet(scalars, own[...], rounded_unit(widened(far)))[0]


def chosen(scalars, outer, inner):
    return jnp.where(scalars[2] > 0.5, widened(outer), widened(inner)).astype(outer.dtype)


def pick_kernel(scalars, outer, inner, whole, out, part):
    out[...] = chosen(scalars, outer, inner)
    part[...] = whole[: part.shape[0]]


def pick_half_kernel(scalars, outer, inner, out):
    half = out.shape[0]
    out[...] = chosen(scalars, outer.at[half:], inner.at[half:])


def last_kernel(count, scalars, own, *refs):
    pieces, (*sums, raw, inverse, out) = refs[:count], refs[count:]
    grad = sum(held[...] for held in sums)
    for piece in pieces:
        grad += meet(scalars, own[...], rounded_unit(widened(piece)))[0]
    finish(out, grad, raw, inverse)


def tied(*values):
    return lax.optimization_barrier(values)


def cost(rows, width, tiles):
    return pl.CostEstimate(
        flops=4 * tiles * rows * rows * width,
        bytes_accessed=12 * tiles * rows * width,
        transcendentals=tiles * rows * rows,
    )


def call(kernel, operands, shapes, rows, width, tiles):
    return pl.pallas_call(
        kernel,
        out_shape=shapes,
        in_specs=[IN_SMEM] + [IN_VMEM] * (len(operands) - 1),
        out_specs=tuple(IN_VMEM for _ in shapes),
        compiler_params=pltpu.CompilerParams(vmem_limit_bytes=VMEM_LIMIT),
        cost_estimate=cost(rows, width, tiles),
    )(*operands)


def on_device(image, text, log_temp, bias):
    rows, width = image.shape
    half = rows // 2
    blocks = lax.axis_size("blk")
    devices = blocks * lax.axis_size("grp")
    place = lax.axis_index("blk") % QUAD
    everyone = range(blocks)
    f32 = jnp.float32
    share = 1.0 / (rows * rows * (2 * REACH + 1) * devices)
    outer = jnp.where((place == 0) | (place == 3), 1.0, 0.0).astype(f32)
    scalars = jnp.stack([jnp.exp(log_temp[0]), bias[0], outer, jnp.full((), share, f32)])

    def send(block, route):
        return lax.ppermute(block, "blk", route)

    beside = [(b, b ^ 1) for b in everyone]
    above = [(b, b ^ 2) for b in everyone]
    beyond = [(b, (b + QUAD if b % QUAD < 2 else b - QUAD) % blocks) for b in everyone]
    def turned(b):
        step = {0: 2, 1: -2, 2: 2, 3: -2}[b % QUAD]
        return (b + step) % blocks

    turn = [(b, turned(b)) for b in everyone]

    tile = jax.ShapeDtypeStruct((rows, width), f32)
    unit = jax.ShapeDtypeStruct((rows, width), jnp.bfloat16)
    part = jax.ShapeDtypeStruct((half, width), jnp.bfloat16)
    column = jax.ShapeDtypeStruct((rows, 128), f32)
    tally = jax.ShapeDtypeStruct((24, 128), f32)
    spread = jax.ShapeDtypeStruct((devices, 4, 128), f32)

    def run(kernel, tiles, operands, *shapes):
        return call(kernel, [scalars, *operands], shapes, rows, width, tiles)

    txt_y = send(text, above)
    txt_x = send(text, beside)
    img_y = send(image, above)
    img_x = send(image, beside)
    img_unit, txt_unit, img_inv, txt_inv, gx, gy, stats = run(
        own_kernel, 2, [image, text], unit, unit, column, column, tile, tile, tally
    )

    txt_y, gx, gy = tied(txt_y, gx, gy)
    txt_z = send(txt_y, beyond)
    gx, stats, unit_y = run(
        text_pair_kernel, 2, [img_unit, txt_y, txt_x, gx, stats], tile, tally, unit
    )
    img_y, gx = tied(img_y, gx)
    img_z = send(img_y, beyond)
    txt_z, img_x, img_y = tied(txt_z, img_x, img_y)
    txt_v, img_h = run(pick_kernel, 1, [txt_y, txt_z, img_x], unit, part)
    txt_w = send(txt_v, beside)
    txt_v, gy = tied(txt_v, gy)
    gy, unit_x = run(image_pair_kernel, 2, [txt_unit, img_y, img_x, gy], tile, unit)
    gx, sums = run(
        text_far_kernel, 2, [img_unit, txt_z, unit_x, unit_y, gx, stats], tile, spread
    )
    img_h, gx = tied(img_h, gx)
    img_k = send(img_h, turn)
    img_z, gx, gy = tied(img_z, gx, gy)
    (img_v,) = run(pick_half_kernel, 1, [img_y, img_z], part)
    img_w = send(img_v, beside)
    sums, txt_w = tied(sums, txt_w)
    seen = lax.all_to_all(sums, ("blk", "grp"), 0, 0)
    statistics = jnp.sum(seen[:, 0, :3], axis=0)
    (far,) = run(image_far_kernel, 1, [txt_unit, img_z], tile)
    far, gx = tied(far, gx)
    (grad_image,) = run(
        functools.partial(last_kernel, 1), 1, [img_unit, txt_w, gx, image, img_inv], tile
    )
    gy, grad_image = tied(gy, grad_image)
    (grad_text,) = run(
        functools.partial(last_kernel, 2),
        1,
        [txt_unit, img_k, img_w, gy, far, text, txt_inv],
        tile,
    )
    return grad_image, grad_text, statistics


def solution(mesh):
    placed = P(("blk", "grp"), None)
    return jax.shard_map(
        on_device,
        mesh=mesh,
        in_specs=(placed, placed, P(), P()),
        out_specs=(placed, placed, P()),
        check_vma=False,
    )
```

```python
import functools

import jax
import jax.numpy as jnp
from jax import lax
from jax.experimental import pallas as pl
from jax.experimental.pallas import tpu as pltpu
from jax.sharding import PartitionSpec as P

REACH = 2
QUAD = 4
VMEM_LIMIT = 16 * 1024 * 1024
IN_VMEM = pl.BlockSpec(memory_space=pltpu.VMEM)
IN_SMEM = pl.BlockSpec(memory_space=pltpu.SMEM)


def unit_rows(raw):
    wide = raw.astype(jnp.float32)
    inverse = 1.0 / jnp.sqrt(jnp.sum(wide * wide, axis=1, keepdims=True) + 1e-06)
    return wide * inverse, inverse


def slopes(similar, temper, offset_bias, diagonal):
    logits = temper * similar + offset_bias
    tail = jnp.exp(-jnp.abs(logits))
    upper = jnp.where(logits >= 0, 1.0, tail) / (1.0 + tail)
    if not diagonal:
        return logits, tail, upper, logits
    lower = jnp.where(logits >= 0, tail, 1.0) / (1.0 + tail)
    same = lax.broadcasted_iota(jnp.int32, similar.shape, 0) == lax.broadcasted_iota(
        jnp.int32, similar.shape, 1
    )
    return logits, tail, jnp.where(same, -lower, upper), jnp.where(same, -logits, logits)


def fold(tile):
    rows, columns = tile.shape
    part = jnp.sum(tile.reshape(rows // 8, 8, columns), axis=0)
    return sum(part[:, c : c + 128] for c in range(0, columns, 128))


def tallies(margin, tail, slope, logits_part):
    pair_loss = jnp.maximum(margin, 0.0) + jnp.log1p(tail)
    return jnp.concatenate([fold(pair_loss), fold(slope * logits_part), fold(slope)], axis=0)


def across(left, right):
    return lax.dot_general(
        left, right, (((1,), (1,)), ((), ())), preferred_element_type=jnp.float32
    )


def own_kernel(scalars, image, text, img_unit, txt_unit, img_inv, txt_inv, gx, gy, stats):
    temper, offset_bias = scalars[0], scalars[1]
    x_wide, x_inv = unit_rows(image[...])
    y_wide, y_inv = unit_rows(text[...])
    x, y = x_wide.astype(jnp.bfloat16), y_wide.astype(jnp.bfloat16)
    img_unit[...] = x
    txt_unit[...] = y
    img_inv[...] = jnp.broadcast_to(x_inv, img_inv.shape)
    txt_inv[...] = jnp.broadcast_to(y_inv, txt_inv.shape)
    similar = across(x, y)
    _, tail, slope, margin = slopes(similar, temper, offset_bias, True)
    stats[...] = tallies(margin, tail, slope, temper * similar)
    scaled = (temper * slope).astype(jnp.bfloat16)
    gx[...] = jnp.dot(scaled, y, preferred_element_type=jnp.float32)
    _, _, slope, _ = slopes(across(y, x), temper, offset_bias, True)
    scaled = (temper * slope).astype(jnp.bfloat16)
    gy[...] = jnp.dot(scaled, x, preferred_element_type=jnp.float32)


def widened(ref):
    return ref[...].astype(jnp.float32)


def rounded_unit(raw):
    return unit_rows(raw)[0].astype(jnp.bfloat16)


def meet(scalars, own, unit, counted=False):
    temper, offset_bias = scalars[0], scalars[1]
    similar = across(own, unit)
    logits, tail, slope, _ = slopes(similar, temper, offset_bias, False)
    scaled = (temper * slope).astype(jnp.bfloat16)
    grad = jnp.dot(scaled, unit, preferred_element_type=jnp.float32)
    tally = tallies(logits, tail, slope, temper * similar) if counted else None
    return grad, tally


def finish(out, grad, raw, inverse):
    inv = inverse[...]
    spans = [slice(c, c + 128) for c in range(0, raw.shape[1], 128)]
    dot = sum(widened(raw.at[:, s]) * grad[:, s] for s in spans)
    pull = jnp.sum(dot, axis=1, keepdims=True) * (inv * inv * inv)
    for s in spans:
        out[:, s] = inv * grad[:, s] - widened(raw.at[:, s]) * pull


def text_pair_kernel(scalars, own, first, second, gx, stats, gx_out, stats_out, unit_out):
    unit = rounded_unit(widened(first))
    unit_out[...] = unit
    grad_a, tally_a = meet(scalars, own[...], unit, True)
    grad_b, tally_b = meet(scalars, own[...], rounded_unit(widened(second)), True)
    gx_out[...] = gx[...] + grad_a + grad_b
    stats_out[...] = stats[...] + tally_a + tally_b


def image_pair_kernel(scalars, own, first, second, gy, gy_out, unit_out, part):
    part[...] = second[: part.shape[0]]
    unit = rounded_unit(widened(second))
    unit_out[...] = unit
    grad_a, _ = meet(scalars, own[...], rounded_unit(widened(first)))
    grad_b, _ = meet(scalars, own[...], unit)
    gy_out[...] = gy[...] + grad_a + grad_b


def text_far_kernel(scalars, own, far, near_image, near_text, gx, stats, gx_out, sums_out):
    temper, offset_bias = scalars[0], scalars[1]
    wide = unit_rows(widened(far))[0]
    grad, tally = meet(scalars, own[...], wide.astype(jnp.bfloat16), True)
    gx_out[...] = gx[...] + grad
    partner = jnp.where(scalars[2] > 0.5, widened(near_text), wide).astype(jnp.bfloat16)
    similar = across(near_image[...], partner)
    logits, tail, slope, _ = slopes(similar, temper, offset_bias, False)
    tally = stats[...] + tally + tallies(logits, tail, slope, temper * similar)
    lane = lax.broadcasted_iota(jnp.int32, (8, 128), 1)
    sums = [jnp.sum(tally[8 * i : 8 * i + 8]) for i in range(3)]
    row = jnp.where(lane == 0, sums[0], jnp.where(lane == 1, sums[1], sums[2]))
    sums_out[...] = jnp.broadcast_to((row * scalars[3])[:4][None], sums_out.shape)


def image_far_kernel(scalars, own, far, out):
    out[...] = meet(scalars, own[...], rounded_unit(widened(far)))[0]


def chosen(scalars, outer, inner):
    return jnp.where(scalars[2] > 0.5, widened(outer), widened(inner)).astype(outer.dtype)


def pick_kernel(scalars, outer, inner, out):
    out[...] = chosen(scalars, outer, inner)


def pick_half_kernel(scalars, outer, inner, out):
    half = out.shape[0]
    out[...] = chosen(scalars, outer.at[half:], inner.at[half:])


def last_kernel(count, scalars, own, *refs):
    pieces, (*sums, raw, inverse, out) = refs[:count], refs[count:]
    grad = sum(held[...] for held in sums)
    for piece in pieces:
        grad += meet(scalars, own[...], rounded_unit(widened(piece)))[0]
    finish(out, grad, raw, inverse)


def tied(*values):
    return lax.optimization_barrier(values)


def cost(rows, width, tiles):
    return pl.CostEstimate(
        flops=4 * tiles * rows * rows * width,
        bytes_accessed=12 * tiles * rows * width,
        transcendentals=tiles * rows * rows,
    )


def call(kernel, operands, shapes, rows, width, tiles):
    return pl.pallas_call(
        kernel,
        out_shape=shapes,
        in_specs=[IN_SMEM] + [IN_VMEM] * (len(operands) - 1),
        out_specs=tuple(IN_VMEM for _ in shapes),
        compiler_params=pltpu.CompilerParams(vmem_limit_bytes=VMEM_LIMIT),
        cost_estimate=cost(rows, width, tiles),
    )(*operands)


def on_device(image, text, log_temp, bias):
    rows, width = image.shape
    half = rows // 2
    blocks = lax.axis_size("blk")
    devices = blocks * lax.axis_size("grp")
    place = lax.axis_index("blk") % QUAD
    everyone = range(blocks)
    f32 = jnp.float32
    share = 1.0 / (rows * rows * (2 * REACH + 1) * devices)
    outer = jnp.where((place == 0) | (place == 3), 1.0, 0.0).astype(f32)
    scalars = jnp.stack([jnp.exp(log_temp[0]), bias[0], outer, jnp.full((), share, f32)])

    def send(block, route):
        return lax.ppermute(block, "blk", route)

    beside = [(b, b ^ 1) for b in everyone]
    above = [(b, b ^ 2) for b in everyone]
    beyond = [(b, (b + QUAD if b % QUAD < 2 else b - QUAD) % blocks) for b in everyone]
    def turned(b):
        step = {0: 2, 1: -2, 2: 2, 3: -2}[b % QUAD]
        return (b + step) % blocks

    turn = [(b, turned(b)) for b in everyone]

    tile = jax.ShapeDtypeStruct((rows, width), f32)
    unit = jax.ShapeDtypeStruct((rows, width), jnp.bfloat16)
    part = jax.ShapeDtypeStruct((half, width), jnp.bfloat16)
    column = jax.ShapeDtypeStruct((rows, 128), f32)
    tally = jax.ShapeDtypeStruct((24, 128), f32)
    spread = jax.ShapeDtypeStruct((devices, 4, 128), f32)

    def run(kernel, tiles, operands, *shapes):
        return call(kernel, [scalars, *operands], shapes, rows, width, tiles)

    txt_y = send(text, above)
    txt_x = send(text, beside)
    img_y = send(image, above)
    img_x = send(image, beside)
    img_unit, txt_unit, img_inv, txt_inv, gx, gy, stats = run(
        own_kernel, 2, [image, text], unit, unit, column, column, tile, tile, tally
    )

    txt_y, gx, gy = tied(txt_y, gx, gy)
    txt_z = send(txt_y, beyond)
    gx, stats, unit_y = run(
        text_pair_kernel, 2, [img_unit, txt_y, txt_x, gx, stats], tile, tally, unit
    )
    img_y, gx = tied(img_y, gx)
    img_z = send(img_y, beyond)
    txt_z, img_x, img_y = tied(txt_z, img_x, img_y)
    (txt_v,) = run(pick_kernel, 1, [txt_y, txt_z], unit)
    txt_w = send(txt_v, beside)
    txt_v, gy = tied(txt_v, gy)
    gy, unit_x, img_h = run(
        image_pair_kernel, 2, [txt_unit, img_y, img_x, gy], tile, unit, part
    )
    gx, sums = run(
        text_far_kernel, 2, [img_unit, txt_z, unit_x, unit_y, gx, stats], tile, spread
    )
    img_h, gx = tied(img_h, gx)
    img_k = send(img_h, turn)
    img_z, gx, gy = tied(img_z, gx, gy)
    (img_v,) = run(pick_half_kernel, 1, [img_y, img_z], part)
    img_w = send(img_v, beside)
    sums, txt_w = tied(sums, txt_w)
    seen = lax.all_to_all(sums, ("blk", "grp"), 0, 0)
    statistics = jnp.sum(seen[:, 0, :3], axis=0)
    (far,) = run(image_far_kernel, 1, [txt_unit, img_z], tile)
    far, gx = tied(far, gx)
    (grad_image,) = run(
        functools.partial(last_kernel, 1), 1, [img_unit, txt_w, gx, image, img_inv], tile
    )
    gy, grad_image = tied(gy, grad_image)
    (grad_text,) = run(
        functools.partial(last_kernel, 2),
        1,
        [txt_unit, img_k, img_w, gy, far, text, txt_inv],
        tile,
    )
    return grad_image, grad_text, statistics


def solution(mesh):
    placed = P(("blk", "grp"), None)
    return jax.shard_map(
        on_device,
        mesh=mesh,
        in_specs=(placed, placed, P(), P()),
        out_specs=(placed, placed, P()),
        check_vma=False,
    )
```

```python
import functools

import jax
import jax.numpy as jnp
from jax import lax
from jax.experimental import pallas as pl
from jax.experimental.pallas import tpu as pltpu
from jax.sharding import PartitionSpec as P

REACH = 2
QUAD = 4
VMEM_LIMIT = 16 * 1024 * 1024
IN_VMEM = pl.BlockSpec(memory_space=pltpu.VMEM)
IN_SMEM = pl.BlockSpec(memory_space=pltpu.SMEM)


def unit_rows(raw):
    wide = raw.astype(jnp.float32)
    inverse = 1.0 / jnp.sqrt(jnp.sum(wide * wide, axis=1, keepdims=True) + 1e-06)
    return wide * inverse, inverse


def slopes(similar, temper, offset_bias, diagonal):
    logits = temper * similar + offset_bias
    tail = jnp.exp(-jnp.abs(logits))
    upper = jnp.where(logits >= 0, 1.0, tail) / (1.0 + tail)
    if not diagonal:
        return logits, tail, upper, logits
    lower = jnp.where(logits >= 0, tail, 1.0) / (1.0 + tail)
    same = lax.broadcasted_iota(jnp.int32, similar.shape, 0) == lax.broadcasted_iota(
        jnp.int32, similar.shape, 1
    )
    return logits, tail, jnp.where(same, -lower, upper), jnp.where(same, -logits, logits)


def fold(tile):
    rows, columns = tile.shape
    part = jnp.sum(tile.reshape(rows // 8, 8, columns), axis=0)
    return sum(part[:, c : c + 128] for c in range(0, columns, 128))


def tallies(margin, tail, slope, logits_part):
    pair_loss = jnp.maximum(margin, 0.0) + jnp.log1p(tail)
    return jnp.concatenate([fold(pair_loss), fold(slope * logits_part), fold(slope)], axis=0)


def across(left, right):
    return lax.dot_general(
        left, right, (((1,), (1,)), ((), ())), preferred_element_type=jnp.float32
    )


def own_kernel(scalars, image, text, img_unit, txt_unit, img_inv, txt_inv, gx, gy, stats):
    temper, offset_bias = scalars[0], scalars[1]
    x_wide, x_inv = unit_rows(image[...])
    y_wide, y_inv = unit_rows(text[...])
    x, y = x_wide.astype(jnp.bfloat16), y_wide.astype(jnp.bfloat16)
    img_unit[...] = x
    txt_unit[...] = y
    img_inv[...] = jnp.broadcast_to(x_inv, img_inv.shape)
    txt_inv[...] = jnp.broadcast_to(y_inv, txt_inv.shape)
    similar = across(x, y)
    _, tail, slope, margin = slopes(similar, temper, offset_bias, True)
    stats[...] = tallies(margin, tail, slope, temper * similar)
    scaled = (temper * slope).astype(jnp.bfloat16)
    gx[...] = jnp.dot(scaled, y, preferred_element_type=jnp.float32)
    _, _, slope, _ = slopes(across(y, x), temper, offset_bias, True)
    scaled = (temper * slope).astype(jnp.bfloat16)
    gy[...] = jnp.dot(scaled, x, preferred_element_type=jnp.float32)


def widened(ref):
    return ref[...].astype(jnp.float32)


def rounded_unit(raw):
    return unit_rows(raw)[0].astype(jnp.bfloat16)


def meet(scalars, own, unit, counted=False):
    temper, offset_bias = scalars[0], scalars[1]
    similar = across(own, unit)
    logits, tail, slope, _ = slopes(similar, temper, offset_bias, False)
    scaled = (temper * slope).astype(jnp.bfloat16)
    grad = jnp.dot(scaled, unit, preferred_element_type=jnp.float32)
    tally = tallies(logits, tail, slope, temper * similar) if counted else None
    return grad, tally


def finish(out, grad, raw, inverse):
    inv = inverse[...]
    spans = [slice(c, c + 128) for c in range(0, raw.shape[1], 128)]
    dot = sum(widened(raw.at[:, s]) * grad[:, s] for s in spans)
    pull = jnp.sum(dot, axis=1, keepdims=True) * (inv * inv * inv)
    for s in spans:
        out[:, s] = inv * grad[:, s] - widened(raw.at[:, s]) * pull


def text_pair_kernel(scalars, own, first, second, gx, stats, gx_out, stats_out, unit_out):
    unit = rounded_unit(widened(first))
    unit_out[...] = unit
    grad_a, tally_a = meet(scalars, own[...], unit, True)
    grad_b, tally_b = meet(scalars, own[...], rounded_unit(widened(second)), True)
    gx_out[...] = gx[...] + grad_a + grad_b
    stats_out[...] = stats[...] + tally_a + tally_b


def image_pair_kernel(scalars, own, first, second, gy, gy_out, unit_out, part):
    part[...] = second[: part.shape[0]]
    unit = rounded_unit(widened(second))
    unit_out[...] = unit
    grad_a, _ = meet(scalars, own[...], rounded_unit(widened(first)))
    grad_b, _ = meet(scalars, own[...], unit)
    gy_out[...] = gy[...] + grad_a + grad_b


def text_far_kernel(scalars, own, far, near_image, near_text, gx, stats, gx_out, sums_out):
    temper, offset_bias = scalars[0], scalars[1]
    wide = unit_rows(widened(far))[0]
    grad, tally = meet(scalars, own[...], wide.astype(jnp.bfloat16), True)
    gx_out[...] = gx[...] + grad
    partner = jnp.where(scalars[2] > 0.5, widened(near_text), wide).astype(jnp.bfloat16)
    similar = across(near_image[...], partner)
    logits, tail, slope, _ = slopes(similar, temper, offset_bias, False)
    tally = stats[...] + tally + tallies(logits, tail, slope, temper * similar)
    lane = lax.broadcasted_iota(jnp.int32, (8, 128), 1)
    sums = [jnp.sum(tally[8 * i : 8 * i + 8]) for i in range(3)]
    row = jnp.where(lane == 0, sums[0], jnp.where(lane == 1, sums[1], sums[2]))
    sums_out[...] = jnp.broadcast_to((row * scalars[3])[:4][None], sums_out.shape)


def image_far_kernel(scalars, own, far, out):
    out[...] = meet(scalars, own[...], rounded_unit(widened(far)))[0]


def chosen(scalars, outer, inner):
    return jnp.where(scalars[2] > 0.5, widened(outer), widened(inner)).astype(outer.dtype)


def pick_kernel(scalars, outer, inner, out):
    out[...] = chosen(scalars, outer, inner)


def pick_half_kernel(scalars, outer, inner, out):
    half = out.shape[0]
    out[...] = chosen(scalars, outer.at[half:], inner.at[half:])


def last_kernel(count, scalars, own, *refs):
    pieces, (*sums, raw, inverse, out) = refs[:count], refs[count:]
    grad = sum(held[...] for held in sums)
    block = jnp.concatenate([widened(piece) for piece in pieces], axis=0)
    grad += meet(scalars, own[...], rounded_unit(block))[0]
    finish(out, grad, raw, inverse)


def tied(*values):
    return lax.optimization_barrier(values)


def cost(rows, width, tiles):
    return pl.CostEstimate(
        flops=4 * tiles * rows * rows * width,
        bytes_accessed=12 * tiles * rows * width,
        transcendentals=tiles * rows * rows,
    )


def call(kernel, operands, shapes, rows, width, tiles):
    return pl.pallas_call(
        kernel,
        out_shape=shapes,
        in_specs=[IN_SMEM] + [IN_VMEM] * (len(operands) - 1),
        out_specs=tuple(IN_VMEM for _ in shapes),
        compiler_params=pltpu.CompilerParams(vmem_limit_bytes=VMEM_LIMIT),
        cost_estimate=cost(rows, width, tiles),
    )(*operands)


def on_device(image, text, log_temp, bias):
    rows, width = image.shape
    half = rows // 2
    blocks = lax.axis_size("blk")
    devices = blocks * lax.axis_size("grp")
    place = lax.axis_index("blk") % QUAD
    everyone = range(blocks)
    f32 = jnp.float32
    share = 1.0 / (rows * rows * (2 * REACH + 1) * devices)
    outer = jnp.where((place == 0) | (place == 3), 1.0, 0.0).astype(f32)
    scalars = jnp.stack([jnp.exp(log_temp[0]), bias[0], outer, jnp.full((), share, f32)])

    def send(block, route):
        return lax.ppermute(block, "blk", route)

    beside = [(b, b ^ 1) for b in everyone]
    above = [(b, b ^ 2) for b in everyone]
    beyond = [(b, (b + QUAD if b % QUAD < 2 else b - QUAD) % blocks) for b in everyone]
    def turned(b):
        step = {0: 2, 1: -2, 2: 2, 3: -2}[b % QUAD]
        return (b + step) % blocks

    turn = [(b, turned(b)) for b in everyone]

    tile = jax.ShapeDtypeStruct((rows, width), f32)
    unit = jax.ShapeDtypeStruct((rows, width), jnp.bfloat16)
    part = jax.ShapeDtypeStruct((half, width), jnp.bfloat16)
    column = jax.ShapeDtypeStruct((rows, 128), f32)
    tally = jax.ShapeDtypeStruct((24, 128), f32)
    spread = jax.ShapeDtypeStruct((devices, 4, 128), f32)

    def run(kernel, tiles, operands, *shapes):
        return call(kernel, [scalars, *operands], shapes, rows, width, tiles)

    txt_y = send(text, above)
    txt_x = send(text, beside)
    img_y = send(image, above)
    img_x = send(image, beside)
    img_unit, txt_unit, img_inv, txt_inv, gx, gy, stats = run(
        own_kernel, 2, [image, text], unit, unit, column, column, tile, tile, tally
    )

    txt_y, gx, gy = tied(txt_y, gx, gy)
    txt_z = send(txt_y, beyond)
    gx, stats, unit_y = run(
        text_pair_kernel, 2, [img_unit, txt_y, txt_x, gx, stats], tile, tally, unit
    )
    img_y, gx = tied(img_y, gx)
    img_z = send(img_y, beyond)
    txt_z, img_x, img_y = tied(txt_z, img_x, img_y)
    (txt_v,) = run(pick_kernel, 1, [txt_y, txt_z], unit)
    txt_w = send(txt_v, beside)
    txt_v, gy = tied(txt_v, gy)
    gy, unit_x, img_h = run(
        image_pair_kernel, 2, [txt_unit, img_y, img_x, gy], tile, unit, part
    )
    gx, sums = run(
        text_far_kernel, 2, [img_unit, txt_z, unit_x, unit_y, gx, stats], tile, spread
    )
    img_h, gx = tied(img_h, gx)
    img_k = send(img_h, turn)
    img_z, gx, gy = tied(img_z, gx, gy)
    (img_v,) = run(pick_half_kernel, 1, [img_y, img_z], part)
    img_w = send(img_v, beside)
    sums, txt_w = tied(sums, txt_w)
    seen = lax.all_to_all(sums, ("blk", "grp"), 0, 0)
    statistics = jnp.sum(seen[:, 0, :3], axis=0)
    (far,) = run(image_far_kernel, 1, [txt_unit, img_z], tile)
    far, gx = tied(far, gx)
    (grad_image,) = run(
        functools.partial(last_kernel, 1), 1, [img_unit, txt_w, gx, image, img_inv], tile
    )
    gy, grad_image = tied(gy, grad_image)
    (grad_text,) = run(
        functools.partial(last_kernel, 2),
        1,
        [txt_unit, img_k, img_w, gy, far, text, txt_inv],
        tile,
    )
    return grad_image, grad_text, statistics


def solution(mesh):
    placed = P(("blk", "grp"), None)
    return jax.shard_map(
        on_device,
        mesh=mesh,
        in_specs=(placed, placed, P(), P()),
        out_specs=(placed, placed, P()),
        check_vma=False,
    )
```
